512 devices in a mesh: ctx: 128 (over x, z, core), head: 4 (over y).
Axes of the slice: x: 4, y: 4, z: 16, core: 2. Of those that a mesh axis runs over, the one named last changes fastest.
Arguments:
- query: bfloat16 [65536, 1024], P('ctx', 'head'), may hold values from -7.5 to 7.5
- key: bfloat16 [65536, 1024], P('ctx', 'head'), may hold values from -7.5 to 7.5
- value: bfloat16 [65536, 1024], P('ctx', 'head'), may hold values from -6 to 6
- grad_out: bfloat16 [65536, 1024], P('ctx', 'head'), may hold values from -6 to 6
- picks: int32 [512, 16, 4], P('ctx', 'head'), may hold values from 0 to 127, as said below
Outputs:
- attn_out: bfloat16 [65536, 1024], P('ctx', 'head')
- grad_query: bfloat16 [65536, 1024], P('ctx', 'head')
- grad_key: bfloat16 [65536, 1024], P('ctx', 'head')
- grad_value: bfloat16 [65536, 1024], P('ctx', 'head')
The draws below stay inside these ranges and needn't reach their ends.
Inputs may be any that keep to these rules, and one draw needn't show every extreme that they name: picks[g, h, 0] is the block that holds tile g; every other entry is that block again (no further block) or an earlier block. Among the tiles of one block and one group of 4 consecutive heads, no earlier block is named twice.
All inputs are finite; a program needn't handle non-finite values.
Results may differ from the reference program's by a relative error of at most 0.017.
Values may be sent and summed in bfloat16 or wider, within the bound.
A program may use at most 64 MiB of HBM per device.

```python
import math
import jax
import jax.numpy as jnp
from jax import lax

HEAD_DIM = 64
HEADS = 16
BLOCK = 512
TILE = 128
TOPK = 4
NBLOCKS = 128
HEAD_GROUPS = 4
HEADS_GRP = 4
TILES_DEV = 4
TOKENS = 65536
TILES = 512


def draw_query(key, part):
    noise = jax.random.normal(jax.random.fold_in(key, 11), (TOKENS, HEADS, HEAD_DIM), jnp.float32)
    noise = 1.5 * noise
    noise = jnp.clip(noise, -7.5, 7.5)
    return noise.reshape(TOKENS, HEADS * HEAD_DIM).astype(jnp.bfloat16)


def draw_key(key, part):
    noise = jax.random.normal(jax.random.fold_in(key, 21), (TOKENS, HEADS, HEAD_DIM), jnp.float32)
    noise = jnp.clip(noise, -7.5, 7.5)
    return noise.reshape(TOKENS, HEADS * HEAD_DIM).astype(jnp.bfloat16)


def draw_picks(key, part):
    tasks = TILES_DEV * HEADS_GRP * (TOPK - 1)
    cap_tasks = max(2 * tasks // 3, 1)
    base = jax.random.fold_in(key, 301)
    key_rank, key_slot = jax.random.split(base)
    owner = jnp.arange(NBLOCKS, dtype=jnp.int32)
    columns = jnp.arange(NBLOCKS, dtype=jnp.int32)
    raw = jax.random.randint(key_rank, (NBLOCKS, HEAD_GROUPS, NBLOCKS), 0, 4096, dtype=jnp.int32)
    score = raw * NBLOCKS + columns[None, None, :]
    score = jnp.where(columns[None, None, :] == 0, 4096 * NBLOCKS + 1, score)
    score = jnp.where(columns[None, None, :] < owner[:, None, None], score, -1 - columns[None, None, :])
    ranking = jnp.argsort(-score, axis=-1).astype(jnp.int32)
    extra = max(tasks - NBLOCKS, 0)
    if extra > 0:
        ranking = jnp.concatenate([ranking, jnp.zeros((NBLOCKS, HEAD_GROUPS, extra), jnp.int32)], axis=-1)
    candidate = ranking[..., :tasks]
    slot_raw = jax.random.randint(key_slot, (NBLOCKS, HEAD_GROUPS, tasks), 0, 4096, dtype=jnp.int32)
    slot_keys = slot_raw * tasks + jnp.arange(tasks, dtype=jnp.int32)[None, None, :]
    permuted = jnp.argsort(slot_keys, axis=-1).astype(jnp.int32)
    chosen = jnp.take_along_axis(candidate, permuted, axis=-1)
    limit = jnp.minimum(owner, cap_tasks)
    active = permuted < limit[:, None, None]
    target = jnp.where(active, chosen, owner[:, None, None])
    target = target.reshape(NBLOCKS, HEAD_GROUPS, TILES_DEV, HEADS_GRP, TOPK - 1)
    leading = jnp.broadcast_to(owner[:, None, None, None, None], (NBLOCKS, HEAD_GROUPS, TILES_DEV, HEADS_GRP, 1))
    full = jnp.concatenate([leading, target], axis=-1)
    full = full.transpose(0, 2, 1, 3, 4).reshape(NBLOCKS * TILES_DEV, HEAD_GROUPS * HEADS_GRP, TOPK)
    return full.astype(jnp.int32)


def level_of(rng, shape, cuts, low, largest):
    loudness, own = 1.0, jax.random.fold_in(rng, 6)
    for dim, shards_of in cuts:
        heights = jnp.exp(jax.random.uniform(jax.random.fold_in(own, dim), (shards_of,), jnp.float32, low / len(cuts), largest / len(cuts)))
        loudness = loudness * jnp.repeat(heights, shape[dim] // shards_of).reshape([-1 if axis == dim else 1 for axis in range(len(shape))])
    return loudness


def gaussian(own_key, extent, scale, bound, pieces=(), kind=jnp.bfloat16):
    drawn = jax.random.normal(own_key, extent, jnp.float32) * scale
    if len(pieces) > 0:
        drawn = level_of(own_key, extent, pieces, -0.22, 0.18) * drawn
    return jnp.clip(drawn, min=-bound, max=bound).astype(kind)


def setup_inputs(seed: int = 0) -> dict:
    streams_of = jax.random.split(jax.random.key(seed), 6)
    return {
        "query": draw_query(jax.random.fold_in(streams_of[5], 71), 0),
        "key": draw_key(jax.random.fold_in(streams_of[5], 71), 0),
        "value": gaussian(streams_of[2], (TOKENS, HEADS * HEAD_DIM), 1.0, 6.0, ((0, 128), (1, 4))),
        "grad_out": gaussian(streams_of[3], (TOKENS, HEADS * HEAD_DIM), 1.0, 6.0, ((0, 128), (1, 4))),
        "picks": draw_picks(jax.random.fold_in(streams_of[5], 71), 0),
    }


masked_value = -1e+30

def reference(query, key, value, grad_out, picks):
    scaling = 1.0 / math.sqrt(HEAD_DIM)
    per_block = BLOCK // TILE
    q_tiles = query.reshape(TILES, TILE, HEADS, HEAD_DIM).transpose(0, 2, 1, 3)
    do_tiles = grad_out.reshape(TILES, TILE, HEADS, HEAD_DIM).transpose(0, 2, 1, 3)
    k_blocks = key.reshape(NBLOCKS, BLOCK, HEADS, HEAD_DIM).transpose(2, 0, 1, 3)
    v_blocks = value.reshape(NBLOCKS, BLOCK, HEADS, HEAD_DIM).transpose(2, 0, 1, 3)
    head_ids = jnp.arange(HEADS, dtype=jnp.int32)[:, None]
    is_first = jnp.arange(TOPK, dtype=jnp.int32) == 0
    key_pos = jnp.arange(BLOCK, dtype=jnp.int32)

    def advance(totals, inputs):
        grad_k, grad_v = totals
        tile_id, q_tile, do_tile, blocks = inputs
        own_block = tile_id // per_block
        is_valid = is_first[None, :] | (blocks != own_block)
        valid_mask = is_valid[:, :, None, None]
        key_rows = k_blocks[head_ids, blocks].astype(jnp.float32)
        value_rows = v_blocks[head_ids, blocks].astype(jnp.float32)
        query_pos = tile_id % per_block * TILE + jnp.arange(TILE, dtype=jnp.int32)
        causal = key_pos[None, :] <= query_pos[:, None]
        allowed = jnp.logical_or(jnp.logical_not(is_first)[:, None, None], causal[None])
        query_wide = q_tile.astype(jnp.float32)
        scores = jnp.einsum('hqd,hikd->hiqk', query_wide, key_rows) * scaling
        scores = jnp.where(allowed[None], scores, masked_value)
        peak_score = lax.optimization_barrier(jnp.max(scores, axis=-1, keepdims=True))
        part_lse = peak_score + jnp.log(lax.optimization_barrier(jnp.sum(jnp.exp(scores - peak_score), axis=-1, keepdims=True)))
        attend = jnp.exp(scores - part_lse)
        attend_low = lax.optimization_barrier(attend.astype(jnp.bfloat16)).astype(jnp.float32)
        part_out = jnp.einsum('hiqk,hikd->hiqd', attend_low, value_rows)
        lse_valid = jnp.where(valid_mask, part_lse, masked_value)
        peak_lse = lax.optimization_barrier(jnp.max(lse_valid, axis=1, keepdims=True))
        total_lse = peak_lse + jnp.log(lax.optimization_barrier(jnp.sum(jnp.exp(lse_valid - peak_lse), axis=1, keepdims=True)))
        weight = jnp.where(valid_mask, jnp.exp(part_lse - total_lse), 0.0)
        out_low = lax.optimization_barrier(lax.optimization_barrier(jnp.sum(weight * part_out, axis=1)).astype(jnp.bfloat16))
        row_delta = lax.optimization_barrier(jnp.sum(do_tile.astype(jnp.float32) * out_low.astype(jnp.float32), axis=-1, keepdims=True))
        scaled = weight * do_tile.astype(jnp.float32)[:, None]
        scaled = lax.optimization_barrier(scaled.astype(jnp.bfloat16)).astype(jnp.float32)
        row_shift = weight * row_delta[:, None]
        part_dv = jnp.einsum('hiqk,hiqd->hikd', attend_low, scaled)
        grad_prob = jnp.einsum('hiqd,hikd->hiqk', scaled, value_rows)
        dscore = attend * (grad_prob - row_shift)
        dscore = lax.optimization_barrier(dscore.astype(jnp.bfloat16)).astype(jnp.float32)
        part_dk = jnp.einsum('hiqk,hqd->hikd', dscore, query_wide) * scaling
        part_dq = lax.optimization_barrier(jnp.sum(jnp.einsum('hiqk,hikd->hiqd', dscore, key_rows) * scaling, axis=1))
        grad_k = grad_k.at[head_ids, blocks].add(part_dk)
        grad_v = grad_v.at[head_ids, blocks].add(part_dv)
        return ((grad_k, grad_v), (out_low, part_dq))
    zeros_kv = jnp.zeros((HEADS, NBLOCKS, BLOCK, HEAD_DIM), jnp.float32)
    tile_ids = jnp.arange(TILES, dtype=jnp.int32)
    totals, outputs = lax.scan(advance, (zeros_kv, zeros_kv), (tile_ids, q_tiles, do_tiles, picks))
    grad_k, grad_v = totals
    out_tiles, dq_tiles = outputs
    attn_out = out_tiles.transpose(0, 2, 1, 3).reshape(TOKENS, HEADS * HEAD_DIM)
    grad_query = dq_tiles.transpose(0, 2, 1, 3).reshape(TOKENS, HEADS * HEAD_DIM).astype(jnp.bfloat16)
    grad_key = grad_k.transpose(1, 2, 0, 3).reshape(TOKENS, HEADS * HEAD_DIM).astype(jnp.bfloat16)
    grad_value = grad_v.transpose(1, 2, 0, 3).reshape(TOKENS, HEADS * HEAD_DIM).astype(jnp.bfloat16)
    return (attn_out, grad_query, grad_key, grad_value)
```

```python
import functools

import jax
import jax.numpy as jnp
from jax import lax
from jax.experimental import pallas as pl
from jax.experimental.pallas import tpu as pltpu
from jax.sharding import PartitionSpec as P

MESH = pl.DeviceIdType.MESH
f32, bf16 = jnp.float32, jnp.bfloat16
HEADS, TILES, DIM, ROWS = 4, 4, 64, 128
TASKS = HEADS * TILES
OTHERS = 3
KEYS = TILES * ROWS
COLS = HEADS * DIM
PAIR = 2 * ROWS
MSG = 2 * DIM + 16
RET = DIM + 16
FAR = -1e30


def dot(a, b):
    return lax.dot_general(a, b, (((1,), (0,)), ((), ())), preferred_element_type=f32)


def dot_rows(a, b):
    return lax.dot_general(a, b, (((1,), (1,)), ((), ())), preferred_element_type=f32)


def kernel(
    n, table, q_ref, k_ref, v_ref, g_ref, ao_ref, dq_ref, dk_ref, dv_ref,
    qg, k8, k8t, vt, kept, inv_sum, sent, got, back, ret, w_sent, w_got, dq_sent, dq_got,
    own_out, own_lse, own_w, w_all, attn, own_dq, dk_acc, dv_acc,
    send_a, send_b, recv_a, recv_b,
):
    me = lax.axis_index("ctx")
    first = (me + 1) // 2
    last = n // 2

    def remote(src, dst, send, recv, peer):
        return pltpu.make_async_remote_copy(
            src_ref=src, dst_ref=dst, send_sem=send.at[peer], recv_sem=recv.at[peer],
            device_id={"ctx": peer}, device_id_type=MESH,
        )

    def push(src, dst, send, recv, peer):
        pltpu.make_async_remote_copy(
            src_ref=src.at[peer], dst_ref=dst.at[me], send_sem=send.at[peer], recv_sem=recv.at[me],
            device_id={"ctx": peer}, device_id_type=MESH,
        ).start()

    barrier = pltpu.get_barrier_semaphore()

    def greet(i, c):
        @pl.when(i != me)
        def _():
            pl.semaphore_signal(barrier, inc=1, device_id={"ctx": i}, device_id_type=MESH)

        return c

    lax.fori_loop(0, n, greet, 0)

    for t in range(TILES):
        rows = slice(t * ROWS, (t + 1) * ROWS)
        q_t = q_ref[rows, :].astype(f32).T.astype(bf16)
        g_t = g_ref[rows, :].astype(f32).T.astype(bf16)
        for h in range(HEADS):
            part = slice(h * DIM, (h + 1) * DIM)
            qg[t * HEADS + h, 0:DIM, :] = q_t[part]
            qg[t * HEADS + h, DIM : 2 * DIM, :] = g_t[part]
        k_rows = k_ref[rows, :].astype(f32) * 0.125
        k8[rows, :] = k_rows.astype(bf16)
        k8t[:, rows] = k_rows.T.astype(bf16)
        vt[:, rows] = v_ref[rows, :].astype(f32).T.astype(bf16)
    got[me, :, :] = jnp.zeros((MSG, ROWS), bf16)
    w_got[me, :, :] = jnp.zeros((2, ROWS), f32)

    pl.semaphore_wait(barrier, n - 1)

    lines = lax.broadcasted_iota(jnp.int32, (16, ROWS), 0)

    def send_tile(j, c):
        d = me - 1 - j
        sent[d, 0 : 2 * DIM, :] = qg[table[0, d]]
        sent[d, 2 * DIM : MSG, :] = jnp.where(lines == table[1, d], 1.0, 0.0).astype(bf16)
        push(sent, got, send_a, recv_a, d)
        return c

    lax.fori_loop(0, me, send_tile, 0)

    def spread(x, mask):
        return jnp.concatenate([(x * mask[h : h + 1]).astype(bf16) for h in range(HEADS)], axis=0)

    def choose(x, mask):
        total = x[0:DIM] * mask[0:1]
        for h in range(1, HEADS):
            total += x[h * DIM : (h + 1) * DIM] * mask[h : h + 1]
        return total

    def own_mask(half):
        row = lax.broadcasted_iota(jnp.int32, (16, PAIR), 0)
        lane = lax.broadcasted_iota(jnp.int32, (16, PAIR), 1)
        return jnp.where(row == 2 * half + lane // ROWS, 1.0, 0.0)

    def two(ref, a, b, start, end):
        return jnp.concatenate([ref[a, start:end, :], ref[b, start:end, :]], axis=1)

    def forward(slot, q_exp, mask, causal=None):
        scores = dot(k8[...], q_exp)
        if causal is not None:
            scores = jnp.where(causal, scores, FAR)
        peak = jnp.max(scores, axis=0, keepdims=True)
        e = jnp.exp(scores - peak)
        total = jnp.sum(e, axis=0, keepdims=True)
        e = e.astype(bf16)
        kept[slot] = e
        over = 1.0 / total
        inv_sum[slot] = over
        out = choose(dot(vt[...], e), mask) * over
        return out, peak + jnp.log(total)

    def backward(slot, q_exp, g_t, mask, w, shift):
        over = inv_sum[slot]
        g_exp = spread((g_t.astype(f32) * (w * over)).astype(bf16).astype(f32), mask)
        e = kept[slot]
        grad_prob = dot(v_ref[...], g_exp)
        dscore = (e.astype(f32) * (grad_prob - shift * over)).astype(bf16)
        dk_acc[...] += dot_rows(dscore, q_exp)
        dv_acc[...] += dot_rows(e, g_exp)
        return choose(dot(k8t[...], dscore), mask)

    def own_forward(t, c):
        key = lax.broadcasted_iota(jnp.int32, (KEYS, PAIR), 0)
        query = lax.broadcasted_iota(jnp.int32, (KEYS, PAIR), 1) % ROWS + t * ROWS
        for half in range(2):
            a = t * HEADS + 2 * half
            mask = own_mask(half)
            q_exp = spread(two(qg, a, a + 1, 0, DIM).astype(f32), mask)
            out, lse = forward(last + 2 * t + half, q_exp, mask, key <= query)
            for i in range(2):
                own_out[a + i] = out[:, i * ROWS : (i + 1) * ROWS]
                own_lse[a + i] = lse[:, i * ROWS : (i + 1) * ROWS]
        return c

    lax.fori_loop(0, TILES, own_forward, 0)

    def serve(j, c):
        a, b = 2 * j, 2 * j + 1

        @pl.when(a > me)
        def _():
            remote(sent.at[a], got.at[a], send_a, recv_a, a).wait_recv()

        remote(sent.at[b], got.at[b], send_a, recv_a, b).wait_recv()
        mask = two(got, a, b, 2 * DIM, MSG).astype(f32)
        q_exp = spread(two(got, a, b, 0, DIM).astype(f32), mask)
        out, lse = forward(j, q_exp, mask)
        high = lse.astype(bf16).astype(f32)
        middle = (lse - high).astype(bf16).astype(f32)
        low = lse - high - middle
        row = lax.broadcasted_iota(jnp.int32, (16, PAIR), 0)
        packed = jnp.where(row == 0, high, jnp.where(row == 1, middle, jnp.where(row == 2, low, 0.0))).astype(bf16)
        out = out.astype(bf16)
        back[a, 0:DIM, :] = out[:, :ROWS]
        back[b, 0:DIM, :] = out[:, ROWS:]
        back[a, DIM:RET, :] = packed[:, :ROWS]
        back[b, DIM:RET, :] = packed[:, ROWS:]

        @pl.when(a > me)
        def _():
            push(back, ret, send_a, recv_a, a)

        push(back, ret, send_a, recv_a, b)
        return c

    lax.fori_loop(first, last, serve, 0)

    def wait_return(d, c):
        remote(back.at[d], ret.at[d], send_a, recv_a, d).wait_recv()
        return c

    lax.fori_loop(0, me, wait_return, 0)

    def combine(th, c):
        parts = []
        lse_own = own_lse[th]
        ceiling = lse_own
        for i in range(OTHERS):
            d = table[3, th * OTHERS + i]
            live = jnp.full((1, ROWS), d, jnp.int32) != me
            terms = ret[d, DIM:RET, :].astype(f32)
            lse = jnp.where(live, terms[0:1] + terms[1:2] + terms[2:3], FAR)
            ceiling = jnp.maximum(ceiling, lse)
            parts.append((d, live, lse))
        total = jnp.exp(lse_own - ceiling)
        for _, _, lse in parts:
            total += jnp.exp(lse - ceiling)
        lse_all = ceiling + jnp.log(total)
        w_own = jnp.exp(lse_own - lse_all)
        mixed = w_own * own_out[th]
        weights = []
        for d, live, lse in parts:
            w = jnp.where(live, jnp.exp(lse - lse_all), 0.0)
            mixed += jnp.where(live, w * ret[d, 0:DIM, :].astype(f32), 0.0)
            weights.append(w)
        low = mixed.astype(bf16).astype(f32)
        delta = jnp.sum(qg[th, DIM : 2 * DIM, :].astype(f32) * low, axis=0, keepdims=True)
        attn[th] = low
        own_w[th] = jnp.concatenate([w_own, w_own * delta], axis=0)
        for i, w in enumerate(weights):
            w_all[th * OTHERS + i] = jnp.concatenate([w, w * delta], axis=0)
        return c

    lax.fori_loop(0, TASKS, combine, 0)

    def send_weights(j, c):
        d = me - 1 - j
        w_sent[d] = w_all[table[2, d]]
        push(w_sent, w_got, send_b, recv_b, d)
        return c

    lax.fori_loop(0, me, send_weights, 0)

    for t in range(TILES):
        block = jnp.concatenate([attn[t * HEADS + h] for h in range(HEADS)], axis=0)
        ao_ref[t * ROWS : (t + 1) * ROWS, :] = block.T.astype(bf16)
    dk_acc[...] = jnp.zeros_like(dk_acc)
    dv_acc[...] = jnp.zeros_like(dv_acc)

    def own_backward(t, c):
        for half in range(2):
            a = t * HEADS + 2 * half
            mask = own_mask(half)
            q_exp = spread(two(qg, a, a + 1, 0, DIM).astype(f32), mask)
            rows = jnp.concatenate([own_w[a], own_w[a + 1]], axis=1)
            grad = backward(
                last + 2 * t + half, q_exp, two(qg, a, a + 1, DIM, 2 * DIM), mask, rows[0:1], rows[1:2]
            )
            for i in range(2):
                own_dq[a + i] = grad[:, i * ROWS : (i + 1) * ROWS]
        return c

    lax.fori_loop(0, TILES, own_backward, 0)

    def serve_back(j, c):
        a, b = 2 * j, 2 * j + 1

        @pl.when(a > me)
        def _():
            remote(w_sent.at[a], w_got.at[a], send_b, recv_b, a).wait_recv()

        remote(w_sent.at[b], w_got.at[b], send_b, recv_b, b).wait_recv()
        mask = two(got, a, b, 2 * DIM, MSG).astype(f32)
        q_exp = spread(two(got, a, b, 0, DIM).astype(f32), mask)
        rows = jnp.concatenate([w_got[a], w_got[b]], axis=1)
        grad = backward(j, q_exp, two(got, a, b, DIM, 2 * DIM), mask, rows[0:1], rows[1:2]).astype(bf16)
        dq_sent[a] = grad[:, :ROWS]
        dq_sent[b] = grad[:, ROWS:]

        @pl.when(a > me)
        def _():
            push(dq_sent, dq_got, send_b, recv_b, a)

        push(dq_sent, dq_got, send_b, recv_b, b)
        return c

    lax.fori_loop(first, last, serve_back, 0)
    dk_ref[...] = (dk_acc[...] * 0.125).astype(bf16)
    dv_ref[...] = dv_acc[...].astype(bf16)

    def wait_down(d, c):
        remote(dq_sent.at[d], dq_got.at[d], send_b, recv_b, d).wait_recv()
        return c

    lax.fori_loop(0, me, wait_down, 0)

    def sum_queries(th, c):
        total = own_dq[th]
        for i in range(OTHERS):
            d = table[3, th * OTHERS + i]
            live = jnp.full((1, ROWS), d, jnp.int32) != me
            total += jnp.where(live, dq_got[d].astype(f32), 0.0)
        own_dq[th] = total
        return c

    lax.fori_loop(0, TASKS, sum_queries, 0)
    for t in range(TILES):
        block = jnp.concatenate([own_dq[t * HEADS + h] for h in range(HEADS)], axis=0)
        dq_ref[t * ROWS : (t + 1) * ROWS, :] = block.T.astype(bf16)

    def drain_low(d, c):
        remote(sent.at[d], got.at[d], send_a, recv_a, d).wait_send()
        remote(w_sent.at[d], w_got.at[d], send_b, recv_b, d).wait_send()
        return c

    def drain_high(s, c):
        remote(back.at[s], ret.at[s], send_a, recv_a, s).wait_send()
        remote(dq_sent.at[s], dq_got.at[s], send_b, recv_b, s).wait_send()
        return c

    lax.fori_loop(0, me, drain_low, 0)
    lax.fori_loop(me + 1, n, drain_high, 0)


def local(query, key, value, grad_out, picks):
    n = lax.axis_size("ctx")
    me = lax.axis_index("ctx")
    targets = picks[:, :, 1:].reshape(TASKS * OTHERS)
    peers = jnp.arange(n, dtype=jnp.int32)
    named = (targets[None, :] == peers[:, None]) & (targets != me)[None, :]
    task = jnp.max(jnp.where(named, jnp.arange(TASKS * OTHERS, dtype=jnp.int32)[None, :], -1), axis=1)
    some = jnp.maximum(task, 0)
    tile_head = some // OTHERS
    width = max(n, TASKS * OTHERS)
    rows = [tile_head, jnp.where(task >= 0, tile_head % HEADS, -1), some, targets]
    table = jnp.stack([jnp.pad(r, (0, width - r.shape[0])) for r in rows])
    shape = jax.ShapeDtypeStruct((KEYS, COLS), bf16)
    vmem = pl.BlockSpec(memory_space=pltpu.VMEM)
    return pl.pallas_call(
        functools.partial(kernel, n),
        out_shape=[shape] * 4,
        in_specs=[pl.BlockSpec(memory_space=pltpu.SMEM)] + [vmem] * 4,
        out_specs=[vmem] * 4,
        scratch_shapes=[
            pltpu.VMEM((TASKS, 2 * DIM, ROWS), bf16),
            pltpu.VMEM((KEYS, COLS), bf16),
            pltpu.VMEM((COLS, KEYS), bf16),
            pltpu.VMEM((COLS, KEYS), bf16),
            pltpu.VMEM((n // 2 + TASKS // 2, KEYS, PAIR), bf16),
            pltpu.VMEM((n // 2 + TASKS // 2, 1, PAIR), f32),
            pltpu.VMEM((n, MSG, ROWS), bf16),
            pltpu.VMEM((n, MSG, ROWS), bf16),
            pltpu.VMEM((n, RET, ROWS), bf16),
            pltpu.VMEM((n, RET, ROWS), bf16),
            pltpu.VMEM((n, 2, ROWS), f32),
            pltpu.VMEM((n, 2, ROWS), f32),
            pltpu.VMEM((n, DIM, ROWS), bf16),
            pltpu.VMEM((n, DIM, ROWS), bf16),
            pltpu.VMEM((TASKS, DIM, ROWS), f32),
            pltpu.VMEM((TASKS, 1, ROWS), f32),
            pltpu.VMEM((TASKS, 2, ROWS), f32),
            pltpu.VMEM((TASKS * OTHERS, 2, ROWS), f32),
            pltpu.VMEM((TASKS, DIM, ROWS), f32),
            pltpu.VMEM((TASKS, DIM, ROWS), f32),
            pltpu.VMEM((KEYS, COLS), f32),
            pltpu.VMEM((KEYS, COLS), f32),
            pltpu.SemaphoreType.DMA((n,)),
            pltpu.SemaphoreType.DMA((n,)),
            pltpu.SemaphoreType.DMA((n,)),
            pltpu.SemaphoreType.DMA((n,)),
        ],
        compiler_params=pltpu.CompilerParams(
            collective_id=0, has_side_effects=True, vmem_limit_bytes=56 * 1024 * 1024
        ),
        name="block_sparse",
    )(table, query, key, value, grad_out)


def solution(mesh):
    whole = P("ctx", "head")
    return jax.shard_map(
        local,
        mesh=mesh,
        in_specs=(whole, whole, whole, whole, P("ctx", "head", None)),
        out_specs=(whole, whole, whole, whole),
        check_vma=False,
    )
```

```python
import functools

import jax
import jax.numpy as jnp
from jax import lax
from jax.experimental import pallas as pl
from jax.experimental.pallas import tpu as pltpu
from jax.sharding import PartitionSpec as P

MESH = pl.DeviceIdType.MESH
f32, bf16 = jnp.float32, jnp.bfloat16
HEADS, TILES, DIM, ROWS = 4, 4, 64, 128
TASKS = HEADS * TILES
OTHERS = 3
KEYS = TILES * ROWS
COLS = HEADS * DIM
PAIR = 2 * ROWS
FAR = -1e30


def dot(a, b):
    return lax.dot_general(a, b, (((1,), (0,)), ((), ())), preferred_element_type=f32)


def dot_rows(a, b):
    return lax.dot_general(a, b, (((1,), (1,)), ((), ())), preferred_element_type=f32)


def kernel(
    n, table, q_ref, k_ref, v_ref, g_ref, ao_ref, dq_ref, dk_ref, dv_ref,
    q_t, g_t, k8, k8t, vt, kept, sent, got, code_sent, code_got, back, ret, lse_sent, lse_got,
    g_all, g_sent, g_got, c_all, c_sent, c_got, dq_sent, dq_got,
    own_out, own_lse, own_g, own_c, attn, own_dq, dk_acc, dv_acc,
    send_a, send_b, send_c, send_d, recv_a, recv_b, recv_c, recv_d,
):
    me = lax.axis_index("ctx")
    first = (me + 1) // 2
    last = n // 2
    quarter = n // 4
    depth = quarter // 2
    my_x, my_z, my_core = me // quarter, (me // 2) % depth, me % 2

    def along(i):
        return jnp.where(i % 2 == 0, i // 2, depth - (i + 1) // 2)

    def peer_of(i):
        x = (my_x + 1 + i // quarter) % 4
        z = (my_z + along((i // 2) % depth)) % depth
        return x * quarter + z * 2 + (my_core + i) % 2

    def source_pair(m):
        x = (my_x + 3 - m % 4) % 4
        return x * depth + (my_z + depth - along(m // 4)) % depth

    def remote(src, dst, send, recv, peer):
        return pltpu.make_async_remote_copy(
            src_ref=src, dst_ref=dst, send_sem=send.at[peer], recv_sem=recv.at[peer],
            device_id={"ctx": peer}, device_id_type=MESH,
        )

    def push(src, dst, send, recv, peer):
        pltpu.make_async_remote_copy(
            src_ref=src.at[peer], dst_ref=dst.at[me], send_sem=send.at[peer], recv_sem=recv.at[me],
            device_id={"ctx": peer}, device_id_type=MESH,
        ).start()

    barrier = pltpu.get_barrier_semaphore()

    def greet(i, c):
        @pl.when(i != me)
        def _():
            pl.semaphore_signal(barrier, inc=1, device_id={"ctx": i}, device_id_type=MESH)

        return c

    lax.fori_loop(0, n, greet, 0)

    for t in range(TILES):
        rows = slice(t * ROWS, (t + 1) * ROWS)
        q_rows = q_ref[rows, :].astype(f32).T.astype(bf16)
        g_rows = g_ref[rows, :].astype(f32).T.astype(bf16)
        for h in range(HEADS):
            part = slice(h * DIM, (h + 1) * DIM)
            q_t[t * HEADS + h] = q_rows[part]
            g_t[t * HEADS + h] = g_rows[part]
        k_rows = k_ref[rows, :].astype(f32) * 0.125
        k8[rows, :] = k_rows.astype(bf16)
        k8t[:, rows] = k_rows.T.astype(bf16)
        vt[:, rows] = v_ref[rows, :].astype(f32).T.astype(bf16)
    got[me] = jnp.zeros((DIM, ROWS), bf16)
    code_got[me] = jnp.full((1, ROWS), -1.0, f32)
    g_got[me] = jnp.zeros((DIM, ROWS), bf16)
    c_got[me] = jnp.zeros((1, ROWS), f32)

    pl.semaphore_wait(barrier, n - 1)

    def send_tile(i, c):
        d = peer_of(i)

        @pl.when(d < me)
        def _():
            sent[d] = q_t[table[0, d]]
            code_sent[d] = jnp.full((1, ROWS), table[1, d], jnp.int32).astype(f32)
            push(code_sent, code_got, send_c, recv_c, d)
            push(sent, got, send_a, recv_a, d)

        return c

    lax.fori_loop(0, n, send_tile, 0)

    def spread(x, mask):
        return jnp.concatenate([(x * mask[h : h + 1]).astype(bf16) for h in range(HEADS)], axis=0)

    def choose(x, mask):
        total = x[0:DIM] * mask[0:1]
        for h in range(1, HEADS):
            total += x[h * DIM : (h + 1) * DIM] * mask[h : h + 1]
        return total

    def own_mask(half):
        row = lax.broadcasted_iota(jnp.int32, (8, PAIR), 0)
        lane = lax.broadcasted_iota(jnp.int32, (8, PAIR), 1)
        return jnp.where(row == 2 * half + lane // ROWS, 1.0, 0.0)

    def two(ref, a, b):
        return jnp.concatenate([ref[a], ref[b]], axis=1)

    def forward(slot, q_exp, mask, causal=None):
        scores = dot(k8[...], q_exp)
        if causal is not None:
            scores = jnp.where(causal, scores, FAR)
        peak = jnp.max(scores, axis=0, keepdims=True)
        e = jnp.exp(scores - peak)
        total = jnp.sum(e, axis=0, keepdims=True)
        e = e.astype(bf16)
        kept[slot] = e
        over = 1.0 / total
        out = choose(dot(vt[...], e), mask) * over
        return out, jnp.concatenate([peak + jnp.log(total), over], axis=0)

    def backward(slot, q_exp, g_exp, mask, shift):
        e = kept[slot]
        grad_prob = dot(v_ref[...], g_exp)
        dscore = (e.astype(f32) * (grad_prob - shift)).astype(bf16)
        dk_acc[...] += dot_rows(dscore, q_exp)
        dv_acc[...] += dot_rows(e, g_exp)
        return choose(dot(k8t[...], dscore), mask)

    def own_forward(t, c):
        key = lax.broadcasted_iota(jnp.int32, (KEYS, PAIR), 0)
        query = lax.broadcasted_iota(jnp.int32, (KEYS, PAIR), 1) % ROWS + t * ROWS
        for half in range(2):
            a = t * HEADS + 2 * half
            mask = own_mask(half)
            q_exp = spread(two(q_t, a, a + 1).astype(f32), mask)
            out, lse = forward(last + 2 * t + half, q_exp, mask, key <= query)
            for i in range(2):
                own_out[a + i] = out[:, i * ROWS : (i + 1) * ROWS]
                own_lse[a + i] = lse[:, i * ROWS : (i + 1) * ROWS]
        return c

    lax.fori_loop(0, TILES, own_forward, 0)

    def masks(a, b):
        code = jnp.concatenate([code_got[a], code_got[b]], axis=1)
        row = lax.broadcasted_iota(jnp.int32, (8, PAIR), 0).astype(f32)
        return jnp.where(row == code, 1.0, 0.0)

    def serve(m, c):
        j = source_pair(m)

        @pl.when(j >= first)
        def _():
            serve_pair(j)

        return c

    def serve_pair(j):
        a, b = 2 * j, 2 * j + 1

        @pl.when(a > me)
        def _():
            remote(code_sent.at[a], code_got.at[a], send_c, recv_c, a).wait_recv()
            remote(sent.at[a], got.at[a], send_a, recv_a, a).wait_recv()

        remote(code_sent.at[b], code_got.at[b], send_c, recv_c, b).wait_recv()
        remote(sent.at[b], got.at[b], send_a, recv_a, b).wait_recv()
        mask = masks(a, b)
        q_exp = spread(two(got, a, b).astype(f32), mask)
        out, lse = forward(j, q_exp, mask)
        out = out.astype(bf16)
        for i, s in enumerate((a, b)):
            back[s] = out[:, i * ROWS : (i + 1) * ROWS]
            lse_sent[s] = lse[:, i * ROWS : (i + 1) * ROWS]

        @pl.when(a > me)
        def _():
            push(lse_sent, lse_got, send_c, recv_c, a)
            push(back, ret, send_a, recv_a, a)

        push(lse_sent, lse_got, send_c, recv_c, b)
        push(back, ret, send_a, recv_a, b)

    lax.fori_loop(0, last, serve, 0)

    def wait_return(d, c):
        remote(lse_sent.at[d], lse_got.at[d], send_c, recv_c, d).wait_recv()
        remote(back.at[d], ret.at[d], send_a, recv_a, d).wait_recv()
        return c

    lax.fori_loop(0, me, wait_return, 0)

    def combine(th, c):
        parts = []
        lse_own = own_lse[th, 0:1, :]
        ceiling = lse_own
        for i in range(OTHERS):
            d = table[3, th * OTHERS + i]
            live = jnp.full((1, ROWS), d, jnp.int32) != me
            rows = lse_got[d]
            lse = jnp.where(live, rows[0:1], FAR)
            ceiling = jnp.maximum(ceiling, lse)
            parts.append((d, live, lse, rows[1:2]))
        total = jnp.exp(lse_own - ceiling)
        for _, _, lse, _ in parts:
            total += jnp.exp(lse - ceiling)
        lse_all = ceiling + jnp.log(total)
        w_own = jnp.exp(lse_own - lse_all)
        mixed = w_own * own_out[th]
        weights = []
        for d, live, lse, over in parts:
            w = jnp.where(live, jnp.exp(lse - lse_all), 0.0)
            mixed += jnp.where(live, w * ret[d].astype(f32), 0.0)
            weights.append(jnp.where(live, w * over, 0.0))
        low = mixed.astype(bf16).astype(f32)
        g = g_t[th].astype(f32)
        delta = jnp.sum(g * low, axis=0, keepdims=True)
        attn[th] = low
        w_own = w_own * own_lse[th, 1:2, :]
        own_g[th] = (w_own * g).astype(bf16)
        own_c[th] = w_own * delta
        for i, w in enumerate(weights):
            g_all[th * OTHERS + i] = (w * g).astype(bf16)
            c_all[th * OTHERS + i] = w * delta
        return c

    lax.fori_loop(0, TASKS, combine, 0)

    def send_grad(i, c):
        d = peer_of(i)

        @pl.when(d < me)
        def _():
            c_sent[d] = c_all[table[2, d]]
            g_sent[d] = g_all[table[2, d]]
            push(c_sent, c_got, send_d, recv_d, d)
            push(g_sent, g_got, send_b, recv_b, d)

        return c

    lax.fori_loop(0, n, send_grad, 0)

    for t in range(TILES):
        block = jnp.concatenate([attn[t * HEADS + h] for h in range(HEADS)], axis=0)
        ao_ref[t * ROWS : (t + 1) * ROWS, :] = block.T.astype(bf16)
    dk_acc[...] = jnp.zeros_like(dk_acc)
    dv_acc[...] = jnp.zeros_like(dv_acc)

    def own_backward(t, c):
        for half in range(2):
            a = t * HEADS + 2 * half
            mask = own_mask(half)
            q_exp = spread(two(q_t, a, a + 1).astype(f32), mask)
            g_exp = spread(two(own_g, a, a + 1).astype(f32), mask)
            grad = backward(last + 2 * t + half, q_exp, g_exp, mask, two(own_c, a, a + 1))
            for i in range(2):
                own_dq[a + i] = grad[:, i * ROWS : (i + 1) * ROWS]
        return c

    lax.fori_loop(0, TILES, own_backward, 0)

    def serve_back(m, c):
        j = source_pair(m)

        @pl.when(j >= first)
        def _():
            serve_back_pair(j)

        return c

    def serve_back_pair(j):
        a, b = 2 * j, 2 * j + 1

        @pl.when(a > me)
        def _():
            remote(c_sent.at[a], c_got.at[a], send_d, recv_d, a).wait_recv()
            remote(g_sent.at[a], g_got.at[a], send_b, recv_b, a).wait_recv()

        remote(c_sent.at[b], c_got.at[b], send_d, recv_d, b).wait_recv()
        remote(g_sent.at[b], g_got.at[b], send_b, recv_b, b).wait_recv()
        mask = masks(a, b)
        q_exp = spread(two(got, a, b).astype(f32), mask)
        g_exp = spread(two(g_got, a, b).astype(f32), mask)
        grad = backward(j, q_exp, g_exp, mask, two(c_got, a, b)).astype(bf16)
        for i, s in enumerate((a, b)):
            dq_sent[s] = grad[:, i * ROWS : (i + 1) * ROWS]

        @pl.when(a > me)
        def _():
            push(dq_sent, dq_got, send_b, recv_b, a)

        push(dq_sent, dq_got, send_b, recv_b, b)

    lax.fori_loop(0, last, serve_back, 0)
    dk_ref[...] = (dk_acc[...] * 0.125).astype(bf16)
    dv_ref[...] = dv_acc[...].astype(bf16)

    def wait_down(d, c):
        remote(dq_sent.at[d], dq_got.at[d], send_b, recv_b, d).wait_recv()
        return c

    lax.fori_loop(0, me, wait_down, 0)

    def sum_queries(th, c):
        total = own_dq[th]
        for i in range(OTHERS):
            d = table[3, th * OTHERS + i]
            live = jnp.full((1, ROWS), d, jnp.int32) != me
            total += jnp.where(live, dq_got[d].astype(f32), 0.0)
        own_dq[th] = total
        return c

    lax.fori_loop(0, TASKS, sum_queries, 0)
    for t in range(TILES):
        block = jnp.concatenate([own_dq[t * HEADS + h] for h in range(HEADS)], axis=0)
        dq_ref[t * ROWS : (t + 1) * ROWS, :] = block.T.astype(bf16)

    def drain_low(d, c):
        remote(code_sent.at[d], code_got.at[d], send_c, recv_c, d).wait_send()
        remote(sent.at[d], got.at[d], send_a, recv_a, d).wait_send()
        remote(c_sent.at[d], c_got.at[d], send_d, recv_d, d).wait_send()
        remote(g_sent.at[d], g_got.at[d], send_b, recv_b, d).wait_send()
        return c

    def drain_high(s, c):
        remote(lse_sent.at[s], lse_got.at[s], send_c, recv_c, s).wait_send()
        remote(back.at[s], ret.at[s], send_a, recv_a, s).wait_send()
        remote(dq_sent.at[s], dq_got.at[s], send_b, recv_b, s).wait_send()
        return c

    lax.fori_loop(0, me, drain_low, 0)
    lax.fori_loop(me + 1, n, drain_high, 0)


def local(query, key, value, grad_out, picks):
    n = lax.axis_size("ctx")
    me = lax.axis_index("ctx")
    targets = picks[:, :, 1:].reshape(TASKS * OTHERS)
    peers = jnp.arange(n, dtype=jnp.int32)
    named = (targets[None, :] == peers[:, None]) & (targets != me)[None, :]
    task = jnp.max(jnp.where(named, jnp.arange(TASKS * OTHERS, dtype=jnp.int32)[None, :], -1), axis=1)
    some = jnp.maximum(task, 0)
    tile_head = some // OTHERS
    width = max(n, TASKS * OTHERS)
    lists = [tile_head, jnp.where(task >= 0, tile_head % HEADS, -1), some, targets]
    table = jnp.stack([jnp.pad(r, (0, width - r.shape[0])) for r in lists])
    shape = jax.ShapeDtypeStruct((KEYS, COLS), bf16)

    def tiles(count, kind=bf16):
        return pltpu.VMEM((count, DIM, ROWS), kind)

    def rows(count, each=1):
        return pltpu.VMEM((count, each, ROWS), f32)

    vmem = pl.BlockSpec(memory_space=pltpu.VMEM)
    return pl.pallas_call(
        functools.partial(kernel, n),
        out_shape=[shape] * 4,
        in_specs=[pl.BlockSpec(memory_space=pltpu.SMEM)] + [vmem] * 4,
        out_specs=[vmem] * 4,
        scratch_shapes=[
            pltpu.VMEM((TASKS, DIM, ROWS), bf16),
            pltpu.VMEM((TASKS, DIM, ROWS), bf16),
            pltpu.VMEM((KEYS, COLS), bf16),
            pltpu.VMEM((COLS, KEYS), bf16),
            pltpu.VMEM((COLS, KEYS), bf16),
            pltpu.VMEM((n // 2 + TASKS // 2, KEYS, PAIR), bf16),
            tiles(n),
            tiles(n),
            rows(n),
            rows(n),
            tiles(n),
            tiles(n),
            rows(n, 2),
            rows(n, 2),
            tiles(TASKS * OTHERS),
            tiles(n),
            tiles(n),
            rows(TASKS * OTHERS),
            rows(n),
            rows(n),
            tiles(n),
            tiles(n),
            tiles(TASKS, f32),
            rows(TASKS, 2),
            tiles(TASKS),
            rows(TASKS),
            tiles(TASKS, f32),
            tiles(TASKS, f32),
            pltpu.VMEM((KEYS, COLS), f32),
            pltpu.VMEM((KEYS, COLS), f32),
            *[pltpu.SemaphoreType.DMA((n,))] * 8,
        ],
        compiler_params=pltpu.CompilerParams(
            collective_id=0, has_side_effects=True, vmem_limit_bytes=56 * 1024 * 1024
        ),
        name="block_sparse",
    )(table, query, key, value, grad_out)


def solution(mesh):
    whole = P("ctx", "head")
    return jax.shard_map(
        local,
        mesh=mesh,
        in_specs=(whole, whole, whole, whole, P("ctx", "head", None)),
        out_specs=(whole, whole, whole, whole),
        check_vma=False,
    )
```

```python
import functools

import jax
import jax.numpy as jnp
from jax import lax
from jax.experimental import pallas as pl
from jax.experimental.pallas import tpu as pltpu
from jax.sharding import PartitionSpec as P

MESH = pl.DeviceIdType.MESH
f32, bf16 = jnp.float32, jnp.bfloat16
HEADS, TILES, DIM, ROWS = 4, 4, 64, 128
TASKS = HEADS * TILES
OTHERS = 3
KEYS = TILES * ROWS
COLS = HEADS * DIM
PAIR = 2 * ROWS
FAR = -1e30
WINDOW = 24


def dot(a, b):
    return lax.dot_general(a, b, (((1,), (0,)), ((), ())), preferred_element_type=f32)


def dot_rows(a, b):
    return lax.dot_general(a, b, (((1,), (1,)), ((), ())), preferred_element_type=f32)


def kernel(
    n, table, q_ref, k_ref, v_ref, g_ref, ao_ref, dq_ref, dk_ref, dv_ref,
    q_t, g_t, k8, k8t, vt, kept, sent, got, code_sent, code_got, back, ret, lse_sent, lse_got,
    g_all, g_sent, g_got, c_all, c_sent, c_got, dq_sent, dq_got,
    own_out, own_lse, own_g, own_c, attn, own_dq, dk_acc, dv_acc,
    send_a, send_b, send_c, send_d, recv_a, recv_b, recv_c, recv_d,
):
    me = lax.axis_index("ctx")
    first = (me + 1) // 2
    last = n // 2
    quarter = n // 4
    depth = quarter // 2
    my_x, my_z, my_core = me // quarter, (me // 2) % depth, me % 2

    def along(i):
        step = i // 2 + i % 2 * (depth // 2)
        return jnp.where(i // 2 % 2 == 0, step, depth - step) % depth

    def peer_of(m, core):
        x = (my_x + 1 + m % 4) % 4
        z = (my_z + along(m // 4)) % depth
        return x * quarter + z * 2 + (my_core + core) % 2

    def source_pair(m):
        x = (my_x + 3 - m % 4) % 4
        return x * depth + (my_z + depth - along(m // 4)) % depth

    def remote(src, dst, send, recv, peer):
        return pltpu.make_async_remote_copy(
            src_ref=src, dst_ref=dst, send_sem=send.at[peer], recv_sem=recv.at[peer],
            device_id={"ctx": peer}, device_id_type=MESH,
        )

    def push(src, dst, send, recv, peer):
        pltpu.make_async_remote_copy(
            src_ref=src.at[peer], dst_ref=dst.at[me], send_sem=send.at[peer], recv_sem=recv.at[me],
            device_id={"ctx": peer}, device_id_type=MESH,
        ).start()

    barrier = pltpu.get_barrier_semaphore()

    def greet(i, c):
        @pl.when(i != me)
        def _():
            pl.semaphore_signal(barrier, inc=1, device_id={"ctx": i}, device_id_type=MESH)

        return c

    lax.fori_loop(0, n, greet, 0)

    for t in range(TILES):
        rows = slice(t * ROWS, (t + 1) * ROWS)
        q_rows = q_ref[rows, :].astype(f32).T.astype(bf16)
        g_rows = g_ref[rows, :].astype(f32).T.astype(bf16)
        for h in range(HEADS):
            part = slice(h * DIM, (h + 1) * DIM)
            q_t[t * HEADS + h] = q_rows[part]
            g_t[t * HEADS + h] = g_rows[part]
        k_rows = k_ref[rows, :].astype(f32) * 0.125
        k8[rows, :] = k_rows.astype(bf16)
        k8t[:, rows] = k_rows.T.astype(bf16)
        vt[:, rows] = v_ref[rows, :].astype(f32).T.astype(bf16)
    got[me] = jnp.zeros((DIM, ROWS), bf16)
    code_got[me] = jnp.full((1, ROWS), -1.0, f32)
    g_got[me] = jnp.zeros((DIM, ROWS), bf16)
    c_got[me] = jnp.zeros((1, ROWS), f32)

    pl.semaphore_wait(barrier, n - 1)

    def send_tile(m, core):
        d = peer_of(m, core)

        @pl.when(d < me)
        def _():
            sent[d] = q_t[table[0, d]]
            code_sent[d] = jnp.full((1, ROWS), table[1, d], jnp.int32).astype(f32)
            push(code_sent, code_got, send_c, recv_c, d)
            push(sent, got, send_a, recv_a, d)

    def spread(x, mask):
        return jnp.concatenate([(x * mask[h : h + 1]).astype(bf16) for h in range(HEADS)], axis=0)

    def choose(x, mask):
        total = x[0:DIM] * mask[0:1]
        for h in range(1, HEADS):
            total += x[h * DIM : (h + 1) * DIM] * mask[h : h + 1]
        return total

    def own_mask(half):
        row = lax.broadcasted_iota(jnp.int32, (8, PAIR), 0)
        lane = lax.broadcasted_iota(jnp.int32, (8, PAIR), 1)
        return jnp.where(row == 2 * half + lane // ROWS, 1.0, 0.0)

    def two(ref, a, b):
        return jnp.concatenate([ref[a], ref[b]], axis=1)

    def forward(slot, q_exp, mask, causal=None):
        scores = dot(k8[...], q_exp)
        if causal is not None:
            scores = jnp.where(causal, scores, FAR)
        peak = jnp.max(scores, axis=0, keepdims=True)
        e = jnp.exp(scores - peak)
        total = jnp.sum(e, axis=0, keepdims=True)
        e = e.astype(bf16)
        kept[slot] = e
        over = 1.0 / total
        out = choose(dot(vt[...], e), mask) * over
        return out, jnp.concatenate([peak + jnp.log(total), over], axis=0)

    def backward(slot, q_exp, g_exp, mask, shift):
        e = kept[slot]
        grad_prob = dot(v_ref[...], g_exp)
        dscore = (e.astype(f32) * (grad_prob - shift)).astype(bf16)
        dk_acc[...] += dot_rows(dscore, q_exp)
        dv_acc[...] += dot_rows(e, g_exp)
        return choose(dot(k8t[...], dscore), mask)

    def own_forward(t, c):
        key = lax.broadcasted_iota(jnp.int32, (KEYS, PAIR), 0)
        query = lax.broadcasted_iota(jnp.int32, (KEYS, PAIR), 1) % ROWS + t * ROWS
        for half in range(2):
            a = t * HEADS + 2 * half
            mask = own_mask(half)
            q_exp = spread(two(q_t, a, a + 1).astype(f32), mask)
            out, lse = forward(last + 2 * t + half, q_exp, mask, key <= query)
            for i in range(2):
                own_out[a + i] = out[:, i * ROWS : (i + 1) * ROWS]
                own_lse[a + i] = lse[:, i * ROWS : (i + 1) * ROWS]
        return c

    def masks(a, b):
        code = jnp.concatenate([code_got[a], code_got[b]], axis=1)
        row = lax.broadcasted_iota(jnp.int32, (8, PAIR), 0).astype(f32)
        return jnp.where(row == code, 1.0, 0.0)

    def serve(m):
        j = source_pair(m)

        @pl.when(j >= first)
        def _():
            serve_pair(j)

    def serve_pair(j):
        a, b = 2 * j, 2 * j + 1

        @pl.when(a > me)
        def _():
            remote(code_sent.at[a], code_got.at[a], send_c, recv_c, a).wait_recv()
            remote(sent.at[a], got.at[a], send_a, recv_a, a).wait_recv()

        remote(code_sent.at[b], code_got.at[b], send_c, recv_c, b).wait_recv()
        remote(sent.at[b], got.at[b], send_a, recv_a, b).wait_recv()
        mask = masks(a, b)
        q_exp = spread(two(got, a, b).astype(f32), mask)
        out, lse = forward(j, q_exp, mask)
        out = out.astype(bf16)
        for i, s in enumerate((a, b)):
            back[s] = out[:, i * ROWS : (i + 1) * ROWS]
            lse_sent[s] = lse[:, i * ROWS : (i + 1) * ROWS]

        @pl.when(a > me)
        def _():
            push(lse_sent, lse_got, send_c, recv_c, a)
            push(back, ret, send_a, recv_a, a)

        push(lse_sent, lse_got, send_c, recv_c, b)
        push(back, ret, send_a, recv_a, b)

    def tile_step(m, c):
        @pl.when(m < last)
        def _():
            for core in range(2):
                send_tile(m, core)

        @pl.when(m == WINDOW - 1)
        def _():
            lax.fori_loop(0, TILES, own_forward, 0)

        @pl.when(m >= WINDOW)
        def _():
            serve(m - WINDOW)

        return c

    lax.fori_loop(0, last + WINDOW, tile_step, 0)

    def wait_return(d, c):
        remote(lse_sent.at[d], lse_got.at[d], send_c, recv_c, d).wait_recv()
        remote(back.at[d], ret.at[d], send_a, recv_a, d).wait_recv()
        return c

    lax.fori_loop(0, me, wait_return, 0)

    def combine(th, c):
        parts = []
        lse_own = own_lse[th, 0:1, :]
        ceiling = lse_own
        for i in range(OTHERS):
            d = table[3, th * OTHERS + i]
            live = jnp.full((1, ROWS), d, jnp.int32) != me
            rows = lse_got[d]
            lse = jnp.where(live, rows[0:1], FAR)
            ceiling = jnp.maximum(ceiling, lse)
            parts.append((d, live, lse, rows[1:2]))
        total = jnp.exp(lse_own - ceiling)
        for _, _, lse, _ in parts:
            total += jnp.exp(lse - ceiling)
        lse_all = ceiling + jnp.log(total)
        w_own = jnp.exp(lse_own - lse_all)
        mixed = w_own * own_out[th]
        weights = []
        for d, live, lse, over in parts:
            w = jnp.where(live, jnp.exp(lse - lse_all), 0.0)
            mixed += jnp.where(live, w * ret[d].astype(f32), 0.0)
            weights.append(jnp.where(live, w * over, 0.0))
        low = mixed.astype(bf16).astype(f32)
        g = g_t[th].astype(f32)
        delta = jnp.sum(g * low, axis=0, keepdims=True)
        attn[th] = low
        w_own = w_own * own_lse[th, 1:2, :]
        own_g[th] = (w_own * g).astype(bf16)
        own_c[th] = w_own * delta
        for i, w in enumerate(weights):
            g_all[th * OTHERS + i] = (w * g).astype(bf16)
            c_all[th * OTHERS + i] = w * delta
        return c

    lax.fori_loop(0, TASKS, combine, 0)

    def send_grad(m, core):
        d = peer_of(m, core)

        @pl.when(d < me)
        def _():
            c_sent[d] = c_all[table[2, d]]
            g_sent[d] = g_all[table[2, d]]
            push(c_sent, c_got, send_d, recv_d, d)
            push(g_sent, g_got, send_b, recv_b, d)

    dk_acc[...] = jnp.zeros_like(dk_acc)
    dv_acc[...] = jnp.zeros_like(dv_acc)

    def own_backward(t, c):
        for half in range(2):
            a = t * HEADS + 2 * half
            mask = own_mask(half)
            q_exp = spread(two(q_t, a, a + 1).astype(f32), mask)
            g_exp = spread(two(own_g, a, a + 1).astype(f32), mask)
            grad = backward(last + 2 * t + half, q_exp, g_exp, mask, two(own_c, a, a + 1))
            for i in range(2):
                own_dq[a + i] = grad[:, i * ROWS : (i + 1) * ROWS]
        return c

    def serve_back(m):
        j = source_pair(m)

        @pl.when(j >= first)
        def _():
            serve_back_pair(j)

    def serve_back_pair(j):
        a, b = 2 * j, 2 * j + 1

        @pl.when(a > me)
        def _():
            remote(c_sent.at[a], c_got.at[a], send_d, recv_d, a).wait_recv()
            remote(g_sent.at[a], g_got.at[a], send_b, recv_b, a).wait_recv()

        remote(c_sent.at[b], c_got.at[b], send_d, recv_d, b).wait_recv()
        remote(g_sent.at[b], g_got.at[b], send_b, recv_b, b).wait_recv()
        mask = masks(a, b)
        q_exp = spread(two(got, a, b).astype(f32), mask)
        g_exp = spread(two(g_got, a, b).astype(f32), mask)
        grad = backward(j, q_exp, g_exp, mask, two(c_got, a, b)).astype(bf16)
        for i, s in enumerate((a, b)):
            dq_sent[s] = grad[:, i * ROWS : (i + 1) * ROWS]

        @pl.when(a > me)
        def _():
            push(dq_sent, dq_got, send_b, recv_b, a)

        push(dq_sent, dq_got, send_b, recv_b, b)

    def grad_step(m, c):
        @pl.when(m < last)
        def _():
            for core in range(2):
                send_grad(m, core)

        @pl.when(m == WINDOW - 1)
        def _():
            for t in range(TILES):
                block = jnp.concatenate([attn[t * HEADS + h] for h in range(HEADS)], axis=0)
                ao_ref[t * ROWS : (t + 1) * ROWS, :] = block.T.astype(bf16)
            lax.fori_loop(0, TILES, own_backward, 0)

        @pl.when(m >= WINDOW)
        def _():
            serve_back(m - WINDOW)

        return c

    lax.fori_loop(0, last + WINDOW, grad_step, 0)
    dk_ref[...] = (dk_acc[...] * 0.125).astype(bf16)
    dv_ref[...] = dv_acc[...].astype(bf16)

    def wait_down(d, c):
        remote(dq_sent.at[d], dq_got.at[d], send_b, recv_b, d).wait_recv()
        return c

    lax.fori_loop(0, me, wait_down, 0)

    def sum_queries(th, c):
        total = own_dq[th]
        for i in range(OTHERS):
            d = table[3, th * OTHERS + i]
            live = jnp.full((1, ROWS), d, jnp.int32) != me
            total += jnp.where(live, dq_got[d].astype(f32), 0.0)
        own_dq[th] = total
        return c

    lax.fori_loop(0, TASKS, sum_queries, 0)
    for t in range(TILES):
        block = jnp.concatenate([own_dq[t * HEADS + h] for h in range(HEADS)], axis=0)
        dq_ref[t * ROWS : (t + 1) * ROWS, :] = block.T.astype(bf16)

    def drain_low(d, c):
        remote(code_sent.at[d], code_got.at[d], send_c, recv_c, d).wait_send()
        remote(sent.at[d], got.at[d], send_a, recv_a, d).wait_send()
        remote(c_sent.at[d], c_got.at[d], send_d, recv_d, d).wait_send()
        remote(g_sent.at[d], g_got.at[d], send_b, recv_b, d).wait_send()
        return c

    def drain_high(s, c):
        remote(lse_sent.at[s], lse_got.at[s], send_c, recv_c, s).wait_send()
        remote(back.at[s], ret.at[s], send_a, recv_a, s).wait_send()
        remote(dq_sent.at[s], dq_got.at[s], send_b, recv_b, s).wait_send()
        return c

    lax.fori_loop(0, me, drain_low, 0)
    lax.fori_loop(me + 1, n, drain_high, 0)


def local(query, key, value, grad_out, picks):
    n = lax.axis_size("ctx")
    me = lax.axis_index("ctx")
    targets = picks[:, :, 1:].reshape(TASKS * OTHERS)
    peers = jnp.arange(n, dtype=jnp.int32)
    named = (targets[None, :] == peers[:, None]) & (targets != me)[None, :]
    task = jnp.max(jnp.where(named, jnp.arange(TASKS * OTHERS, dtype=jnp.int32)[None, :], -1), axis=1)
    some = jnp.maximum(task, 0)
    tile_head = some // OTHERS
    width = max(n, TASKS * OTHERS)
    lists = [tile_head, jnp.where(task >= 0, tile_head % HEADS, -1), some, targets]
    table = jnp.stack([jnp.pad(r, (0, width - r.shape[0])) for r in lists])
    shape = jax.ShapeDtypeStruct((KEYS, COLS), bf16)

    def tiles(count, kind=bf16):
        return pltpu.VMEM((count, DIM, ROWS), kind)

    def rows(count, each=1):
        return pltpu.VMEM((count, each, ROWS), f32)

    vmem = pl.BlockSpec(memory_space=pltpu.VMEM)
    return pl.pallas_call(
        functools.partial(kernel, n),
        out_shape=[shape] * 4,
        in_specs=[pl.BlockSpec(memory_space=pltpu.SMEM)] + [vmem] * 4,
        out_specs=[vmem] * 4,
        scratch_shapes=[
            pltpu.VMEM((TASKS, DIM, ROWS), bf16),
            pltpu.VMEM((TASKS, DIM, ROWS), bf16),
            pltpu.VMEM((KEYS, COLS), bf16),
            pltpu.VMEM((COLS, KEYS), bf16),
            pltpu.VMEM((COLS, KEYS), bf16),
            pltpu.VMEM((n // 2 + TASKS // 2, KEYS, PAIR), bf16),
            tiles(n),
            tiles(n),
            rows(n),
            rows(n),
            tiles(n),
            tiles(n),
            rows(n, 2),
            rows(n, 2),
            tiles(TASKS * OTHERS),
            tiles(n),
            tiles(n),
            rows(TASKS * OTHERS),
            rows(n),
            rows(n),
            tiles(n),
            tiles(n),
            tiles(TASKS, f32),
            rows(TASKS, 2),
            tiles(TASKS),
            rows(TASKS),
            tiles(TASKS, f32),
            tiles(TASKS, f32),
            pltpu.VMEM((KEYS, COLS), f32),
            pltpu.VMEM((KEYS, COLS), f32),
            *[pltpu.SemaphoreType.DMA((n,))] * 8,
        ],
        compiler_params=pltpu.CompilerParams(
            collective_id=0, has_side_effects=True, vmem_limit_bytes=56 * 1024 * 1024
        ),
        name="block_sparse",
    )(table, query, key, value, grad_out)


def solution(mesh):
    whole = P("ctx", "head")
    return jax.shard_map(
        local,
        mesh=mesh,
        in_specs=(whole, whole, whole, whole, P("ctx", "head", None)),
        out_specs=(whole, whole, whole, whole),
        check_vma=False,
    )
```

```python
import functools

import jax
import jax.numpy as jnp
from jax import lax
from jax.experimental import pallas as pl
from jax.experimental.pallas import tpu as pltpu
from jax.sharding import PartitionSpec as P

MESH = pl.DeviceIdType.MESH
f32, bf16 = jnp.float32, jnp.bfloat16
HEADS, TILES, DIM, ROWS = 4, 4, 64, 128
TASKS = HEADS * TILES
OTHERS = 3
KEYS = TILES * ROWS
COLS = HEADS * DIM
PAIR = 2 * ROWS
FAR = -1e30
LATE = 4
WINDOW = 16


def dot(a, b):
    return lax.dot_general(a, b, (((1,), (0,)), ((), ())), preferred_element_type=f32)


def dot_rows(a, b):
    return lax.dot_general(a, b, (((1,), (1,)), ((), ())), preferred_element_type=f32)


def kernel(
    n, table, q_ref, k_ref, v_ref, g_ref, ao_ref, dq_ref, dk_ref, dv_ref,
    q_t, g_t, k8, k8t, vt, kept, sent, got, code_sent, code_got, back, ret, lse_sent, lse_got,
    g_all, g_sent, g_got, c_all, c_sent, c_got, dq_sent, dq_got,
    own_out, own_lse, own_g, own_c, attn, own_dq, dk_acc, dv_acc,
    send_a, send_b, send_c, send_d, recv_a, recv_b, recv_c, recv_d,
):
    me = lax.axis_index("ctx")
    first = (me + 1) // 2
    last = n // 2
    quarter = n // 4
    depth = quarter // 2
    my_x, my_z, my_core = me // quarter, (me // 2) % depth, me % 2

    def along(i):
        step = i // 2 + i % 2 * (depth // 2)
        return jnp.where(i // 2 % 2 == 0, step, depth - step) % depth

    def peer_of(m, core):
        x = (my_x + 1 + m % 4) % 4
        z = (my_z + along(m // 4)) % depth
        return x * quarter + z * 2 + (my_core + core) % 2

    def source_pair(m):
        x = (my_x + 3 - m % 4) % 4
        zz = m // 4 - jnp.where(x == 3, LATE, 0)
        j = x * depth + (my_z + 2 * depth - along(jnp.clip(zz, 0, depth - 1))) % depth
        return j, (zz >= 0) & (zz < depth) & (j >= first)

    def remote(src, dst, send, recv, peer):
        return pltpu.make_async_remote_copy(
            src_ref=src, dst_ref=dst, send_sem=send.at[peer], recv_sem=recv.at[peer],
            device_id={"ctx": peer}, device_id_type=MESH,
        )

    def push(src, dst, send, recv, peer):
        pltpu.make_async_remote_copy(
            src_ref=src.at[peer], dst_ref=dst.at[me], send_sem=send.at[peer], recv_sem=recv.at[me],
            device_id={"ctx": peer}, device_id_type=MESH,
        ).start()

    barrier = pltpu.get_barrier_semaphore()

    def greet(i, c):
        @pl.when(i != me)
        def _():
            pl.semaphore_signal(barrier, inc=1, device_id={"ctx": i}, device_id_type=MESH)

        return c

    lax.fori_loop(0, n, greet, 0)

    for t in range(TILES):
        rows = slice(t * ROWS, (t + 1) * ROWS)
        q_rows = q_ref[rows, :].astype(f32).T.astype(bf16)
        g_rows = g_ref[rows, :].astype(f32).T.astype(bf16)
        for h in range(HEADS):
            part = slice(h * DIM, (h + 1) * DIM)
            q_t[t * HEADS + h] = q_rows[part]
            g_t[t * HEADS + h] = g_rows[part]
        k_rows = k_ref[rows, :].astype(f32) * 0.125
        k8[rows, :] = k_rows.astype(bf16)
        k8t[:, rows] = k_rows.T.astype(bf16)
        vt[:, rows] = v_ref[rows, :].astype(f32).T.astype(bf16)
    got[me] = jnp.zeros((DIM, ROWS), bf16)
    code_got[me] = jnp.full((1, ROWS), -1.0, f32)
    g_got[me] = jnp.zeros((DIM, ROWS), bf16)
    c_got[me] = jnp.zeros((1, ROWS), f32)

    pl.semaphore_wait(barrier, n - 1)

    def send_tile(m, core):
        d = peer_of(m, core)

        @pl.when(d < me)
        def _():
            sent[d] = q_t[table[0, d]]
            code_sent[d] = jnp.full((1, ROWS), table[1, d], jnp.int32).astype(f32)
            push(code_sent, code_got, send_c, recv_c, d)
            push(sent, got, send_a, recv_a, d)

    def spread(x, mask):
        return jnp.concatenate([(x * mask[h : h + 1]).astype(bf16) for h in range(HEADS)], axis=0)

    def choose(x, mask):
        total = x[0:DIM] * mask[0:1]
        for h in range(1, HEADS):
            total += x[h * DIM : (h + 1) * DIM] * mask[h : h + 1]
        return total

    def own_mask(half):
        row = lax.broadcasted_iota(jnp.int32, (8, PAIR), 0)
        lane = lax.broadcasted_iota(jnp.int32, (8, PAIR), 1)
        return jnp.where(row == 2 * half + lane // ROWS, 1.0, 0.0)

    def two(ref, a, b):
        return jnp.concatenate([ref[a], ref[b]], axis=1)

    def forward(slot, q_exp, mask, causal=None):
        scores = dot(k8[...], q_exp)
        if causal is not None:
            scores = jnp.where(causal, scores, FAR)
        peak = jnp.max(scores, axis=0, keepdims=True)
        e = jnp.exp(scores - peak)
        total = jnp.sum(e, axis=0, keepdims=True)
        e = e.astype(bf16)
        kept[slot] = e
        over = 1.0 / total
        out = choose(dot(vt[...], e), mask) * over
        return out, jnp.concatenate([peak + jnp.log(total), over], axis=0)

    def backward(slot, q_exp, g_exp, mask, shift):
        e = kept[slot]
        grad_prob = dot(v_ref[...], g_exp)
        dscore = (e.astype(f32) * (grad_prob - shift)).astype(bf16)
        dk_acc[...] += dot_rows(dscore, q_exp)
        dv_acc[...] += dot_rows(e, g_exp)
        return choose(dot(k8t[...], dscore), mask)

    def own_forward(t, c):
        key = lax.broadcasted_iota(jnp.int32, (KEYS, PAIR), 0)
        query = lax.broadcasted_iota(jnp.int32, (KEYS, PAIR), 1) % ROWS + t * ROWS
        for half in range(2):
            a = t * HEADS + 2 * half
            mask = own_mask(half)
            q_exp = spread(two(q_t, a, a + 1).astype(f32), mask)
            out, lse = forward(last + 2 * t + half, q_exp, mask, key <= query)
            for i in range(2):
                own_out[a + i] = out[:, i * ROWS : (i + 1) * ROWS]
                own_lse[a + i] = lse[:, i * ROWS : (i + 1) * ROWS]
        return c

    def masks(a, b):
        code = jnp.concatenate([code_got[a], code_got[b]], axis=1)
        row = lax.broadcasted_iota(jnp.int32, (8, PAIR), 0).astype(f32)
        return jnp.where(row == code, 1.0, 0.0)

    def serve(m):
        j, live = source_pair(m)

        @pl.when(live)
        def _():
            serve_pair(j)

    def serve_pair(j):
        a, b = 2 * j, 2 * j + 1

        @pl.when(a > me)
        def _():
            remote(code_sent.at[a], code_got.at[a], send_c, recv_c, a).wait_recv()
            remote(sent.at[a], got.at[a], send_a, recv_a, a).wait_recv()

        remote(code_sent.at[b], code_got.at[b], send_c, recv_c, b).wait_recv()
        remote(sent.at[b], got.at[b], send_a, recv_a, b).wait_recv()
        mask = masks(a, b)
        q_exp = spread(two(got, a, b).astype(f32), mask)
        out, lse = forward(j, q_exp, mask)
        out = out.astype(bf16)
        for i, s in enumerate((a, b)):
            back[s] = out[:, i * ROWS : (i + 1) * ROWS]
            lse_sent[s] = lse[:, i * ROWS : (i + 1) * ROWS]

        @pl.when(a > me)
        def _():
            push(lse_sent, lse_got, send_c, recv_c, a)
            push(back, ret, send_a, recv_a, a)

        push(lse_sent, lse_got, send_c, recv_c, b)
        push(back, ret, send_a, recv_a, b)

    def tile_step(m, c):
        @pl.when(m < last)
        def _():
            for core in range(2):
                send_tile(m, core)

        @pl.when(m == WINDOW - 1)
        def _():
            lax.fori_loop(0, TILES, own_forward, 0)

        @pl.when(m >= WINDOW)
        def _():
            serve(m - WINDOW)

        return c

    lax.fori_loop(0, last + 4 * LATE + WINDOW, tile_step, 0)

    def wait_return(d, c):
        remote(lse_sent.at[d], lse_got.at[d], send_c, recv_c, d).wait_recv()
        remote(back.at[d], ret.at[d], send_a, recv_a, d).wait_recv()
        return c

    lax.fori_loop(0, me, wait_return, 0)

    def combine(th, c):
        parts = []
        lse_own = own_lse[th, 0:1, :]
        ceiling = lse_own
        for i in range(OTHERS):
            d = table[3, th * OTHERS + i]
            live = jnp.full((1, ROWS), d, jnp.int32) != me
            rows = lse_got[d]
            lse = jnp.where(live, rows[0:1], FAR)
            ceiling = jnp.maximum(ceiling, lse)
            parts.append((d, live, lse, rows[1:2]))
        total = jnp.exp(lse_own - ceiling)
        for _, _, lse, _ in parts:
            total += jnp.exp(lse - ceiling)
        lse_all = ceiling + jnp.log(total)
        w_own = jnp.exp(lse_own - lse_all)
        mixed = w_own * own_out[th]
        weights = []
        for d, live, lse, over in parts:
            w = jnp.where(live, jnp.exp(lse - lse_all), 0.0)
            mixed += jnp.where(live, w * ret[d].astype(f32), 0.0)
            weights.append(jnp.where(live, w * over, 0.0))
        low = mixed.astype(bf16).astype(f32)
        g = g_t[th].astype(f32)
        delta = jnp.sum(g * low, axis=0, keepdims=True)
        attn[th] = low
        w_own = w_own * own_lse[th, 1:2, :]
        own_g[th] = (w_own * g).astype(bf16)
        own_c[th] = w_own * delta
        for i, w in enumerate(weights):
            g_all[th * OTHERS + i] = (w * g).astype(bf16)
            c_all[th * OTHERS + i] = w * delta
        return c

    lax.fori_loop(0, TASKS, combine, 0)

    def send_grad(m, core):
        d = peer_of(m, core)

        @pl.when(d < me)
        def _():
            c_sent[d] = c_all[table[2, d]]
            g_sent[d] = g_all[table[2, d]]
            push(c_sent, c_got, send_d, recv_d, d)
            push(g_sent, g_got, send_b, recv_b, d)

    dk_acc[...] = jnp.zeros_like(dk_acc)
    dv_acc[...] = jnp.zeros_like(dv_acc)

    def own_backward(t, c):
        for half in range(2):
            a = t * HEADS + 2 * half
            mask = own_mask(half)
            q_exp = spread(two(q_t, a, a + 1).astype(f32), mask)
            g_exp = spread(two(own_g, a, a + 1).astype(f32), mask)
            grad = backward(last + 2 * t + half, q_exp, g_exp, mask, two(own_c, a, a + 1))
            for i in range(2):
                own_dq[a + i] = grad[:, i * ROWS : (i + 1) * ROWS]
        return c

    def serve_back(m):
        j, live = source_pair(m)

        @pl.when(live)
        def _():
            serve_back_pair(j)

    def serve_back_pair(j):
        a, b = 2 * j, 2 * j + 1

        @pl.when(a > me)
        def _():
            remote(c_sent.at[a], c_got.at[a], send_d, recv_d, a).wait_recv()
            remote(g_sent.at[a], g_got.at[a], send_b, recv_b, a).wait_recv()

        remote(c_sent.at[b], c_got.at[b], send_d, recv_d, b).wait_recv()
        remote(g_sent.at[b], g_got.at[b], send_b, recv_b, b).wait_recv()
        mask = masks(a, b)
        q_exp = spread(two(got, a, b).astype(f32), mask)
        g_exp = spread(two(g_got, a, b).astype(f32), mask)
        grad = backward(j, q_exp, g_exp, mask, two(c_got, a, b)).astype(bf16)
        for i, s in enumerate((a, b)):
            dq_sent[s] = grad[:, i * ROWS : (i + 1) * ROWS]

        @pl.when(a > me)
        def _():
            push(dq_sent, dq_got, send_b, recv_b, a)

        push(dq_sent, dq_got, send_b, recv_b, b)

    def grad_step(m, c):
        @pl.when(m < last)
        def _():
            for core in range(2):
                send_grad(m, core)

        @pl.when(m == WINDOW - 1)
        def _():
            for t in range(TILES):
                block = jnp.concatenate([attn[t * HEADS + h] for h in range(HEADS)], axis=0)
                ao_ref[t * ROWS : (t + 1) * ROWS, :] = block.T.astype(bf16)
            lax.fori_loop(0, TILES, own_backward, 0)

        @pl.when(m >= WINDOW)
        def _():
            serve_back(m - WINDOW)

        return c

    lax.fori_loop(0, last + 4 * LATE + WINDOW, grad_step, 0)
    dk_ref[...] = (dk_acc[...] * 0.125).astype(bf16)
    dv_ref[...] = dv_acc[...].astype(bf16)

    def wait_down(d, c):
        remote(dq_sent.at[d], dq_got.at[d], send_b, recv_b, d).wait_recv()
        return c

    lax.fori_loop(0, me, wait_down, 0)

    def sum_queries(th, c):
        total = own_dq[th]
        for i in range(OTHERS):
            d = table[3, th * OTHERS + i]
            live = jnp.full((1, ROWS), d, jnp.int32) != me
            total += jnp.where(live, dq_got[d].astype(f32), 0.0)
        own_dq[th] = total
        return c

    lax.fori_loop(0, TASKS, sum_queries, 0)
    for t in range(TILES):
        block = jnp.concatenate([own_dq[t * HEADS + h] for h in range(HEADS)], axis=0)
        dq_ref[t * ROWS : (t + 1) * ROWS, :] = block.T.astype(bf16)

    def drain_low(d, c):
        remote(code_sent.at[d], code_got.at[d], send_c, recv_c, d).wait_send()
        remote(sent.at[d], got.at[d], send_a, recv_a, d).wait_send()
        remote(c_sent.at[d], c_got.at[d], send_d, recv_d, d).wait_send()
        remote(g_sent.at[d], g_got.at[d], send_b, recv_b, d).wait_send()
        return c

    def drain_high(s, c):
        remote(lse_sent.at[s], lse_got.at[s], send_c, recv_c, s).wait_send()
        remote(back.at[s], ret.at[s], send_a, recv_a, s).wait_send()
        remote(dq_sent.at[s], dq_got.at[s], send_b, recv_b, s).wait_send()
        return c

    lax.fori_loop(0, me, drain_low, 0)
    lax.fori_loop(me + 1, n, drain_high, 0)


def local(query, key, value, grad_out, picks):
    n = lax.axis_size("ctx")
    me = lax.axis_index("ctx")
    targets = picks[:, :, 1:].reshape(TASKS * OTHERS)
    peers = jnp.arange(n, dtype=jnp.int32)
    named = (targets[None, :] == peers[:, None]) & (targets != me)[None, :]
    task = jnp.max(jnp.where(named, jnp.arange(TASKS * OTHERS, dtype=jnp.int32)[None, :], -1), axis=1)
    some = jnp.maximum(task, 0)
    tile_head = some // OTHERS
    width = max(n, TASKS * OTHERS)
    lists = [tile_head, jnp.where(task >= 0, tile_head % HEADS, -1), some, targets]
    table = jnp.stack([jnp.pad(r, (0, width - r.shape[0])) for r in lists])
    shape = jax.ShapeDtypeStruct((KEYS, COLS), bf16)

    def tiles(count, kind=bf16):
        return pltpu.VMEM((count, DIM, ROWS), kind)

    def rows(count, each=1):
        return pltpu.VMEM((count, each, ROWS), f32)

    vmem = pl.BlockSpec(memory_space=pltpu.VMEM)
    return pl.pallas_call(
        functools.partial(kernel, n),
        out_shape=[shape] * 4,
        in_specs=[pl.BlockSpec(memory_space=pltpu.SMEM)] + [vmem] * 4,
        out_specs=[vmem] * 4,
        scratch_shapes=[
            pltpu.VMEM((TASKS, DIM, ROWS), bf16),
            pltpu.VMEM((TASKS, DIM, ROWS), bf16),
            pltpu.VMEM((KEYS, COLS), bf16),
            pltpu.VMEM((COLS, KEYS), bf16),
            pltpu.VMEM((COLS, KEYS), bf16),
            pltpu.VMEM((n // 2 + TASKS // 2, KEYS, PAIR), bf16),
            tiles(n),
            tiles(n),
            rows(n),
            rows(n),
            tiles(n),
            tiles(n),
            rows(n, 2),
            rows(n, 2),
            tiles(TASKS * OTHERS),
            tiles(n),
            tiles(n),
            rows(TASKS * OTHERS),
            rows(n),
            rows(n),
            tiles(n),
            tiles(n),
            tiles(TASKS, f32),
            rows(TASKS, 2),
            tiles(TASKS),
            rows(TASKS),
            tiles(TASKS, f32),
            tiles(TASKS, f32),
            pltpu.VMEM((KEYS, COLS), f32),
            pltpu.VMEM((KEYS, COLS), f32),
            *[pltpu.SemaphoreType.DMA((n,))] * 8,
        ],
        compiler_params=pltpu.CompilerParams(
            collective_id=0, has_side_effects=True, vmem_limit_bytes=56 * 1024 * 1024
        ),
        name="block_sparse",
    )(table, query, key, value, grad_out)


def solution(mesh):
    whole = P("ctx", "head")
    return jax.shard_map(
        local,
        mesh=mesh,
        in_specs=(whole, whole, whole, whole, P("ctx", "head", None)),
        out_specs=(whole, whole, whole, whole),
        check_vma=False,
    )
```
